32 devices in a mesh: tensor: 4 (over x, core), expert: 4 (over z), dp: 2 (over y).
Axes of the slice: x: 2, y: 2, z: 4, core: 2. Of those that a mesh axis runs over, the one named last changes fastest.
Arguments:
- queries: bfloat16 [8, 256, 2, 4096], P(('dp', 'expert'), None, None, 'tensor'), parts along dimension 0, may hold values from -6 to 6
- keys: bfloat16 [8, 256, 2, 512], P(('dp', 'expert'), None, None, 'tensor'), parts along dimension 0, may hold values from -6 to 6
- values: bfloat16 [8, 256, 2, 512], P(('dp', 'expert'), None, None, 'tensor'), parts along dimension 0, may hold values from -12 to 12
- q_gain: float32 [128], replicated, may hold values from 0 to 7
- k_gain: float32 [128], replicated, may hold values from 0 to 7
- out_weight: bfloat16 [4096, 4096], P('tensor', 'expert'), may hold values from -0.09375 to 0.09375
- hidden_in: bfloat16 [8, 256, 2, 4096], P(('dp', 'expert'), 'tensor'), parts along dimension 0, may hold values from -3 to 3
- norm_gain: float32 [4096], replicated, may hold values from 0.1 to 1.9
- router: bfloat16 [4096, 16], replicated, may hold values from -4 to 4
- expert_ids: int32 [8, 256, 2, 8], P(('dp', 'expert'), 'tensor'), parts along dimension 0, may hold values from 0 to 15, all different within a row; in each aligned block of 128 rows (0 to 127, 128 to 255, ..., all dimensions but the last counted through in order) at most 65 rows name the same one
- w_gate: bfloat16 [16, 4096, 768], P(('tensor', 'expert')), may hold values from -0.09375 to 0.09375
- w_up: bfloat16 [16, 4096, 768], P(('tensor', 'expert')), may hold values from -0.09375 to 0.09375
- w_down: bfloat16 [16, 768, 4096], P(('tensor', 'expert')), may hold values from -0.21875 to 0.21875
Outputs:
- hidden_out: bfloat16 [8, 256, 2, 4096], P(('dp', 'expert'), 'tensor'), parts along dimension 0
The draws below stay inside these ranges and needn't reach their ends.
There are 2 independent parts, one for each index of `dp`. The reference program is written for one: setup_inputs(seed, part) draws one part's arguments, and reference() takes and returns one part's arrays. A program takes and returns all parts, laid end to end along the dimension named above; an argument that names none is the same for every part. Nothing has to cross between parts.
Inputs may be any that keep to these rules, and one draw needn't show every extreme that they name: `expert_ids`: each row names 8 different experts; among the 128 rows of one device no expert is named by more than 65 rows, a bound that some block reaches.
All inputs are finite; a program needn't handle non-finite values.
Results may differ from the reference program's by a relative error of at most 0.03.
The reference program's roundings to bfloat16 on the way count: a program that leaves them out, or rounds other values in their place, can miss the bound.
Values may be sent and summed in bfloat16 or wider, within the bound.
A program may use at most 256 MiB of HBM per device.

```python
import math
import jax
import jax.numpy as jnp
import numpy as np
from jax import lax

D = 4096
HD = 128
FF = 768
TOPK = 8
SEQS = 2
HEADS = 32
KV_HEADS = 4
EXPERTS = 16
BLOCK = 256
BLOCKS = 4
ROWS_DEV = 128
CAP = 65


def draw_q_gain(key, part):
    folded = jax.random.fold_in(key, 11)
    result = jax.random.uniform(folded, (HD,), jnp.float32, 0.5, 2.0)
    return result


def draw_k_gain(key, part):
    folded = jax.random.fold_in(key, 23)
    result = jax.random.uniform(folded, (HD,), jnp.float32, 0.5, 2.0)
    return result


def draw_router(key, part):
    folded = jax.random.fold_in(key, 37)
    spread = jax.random.normal(folded, (D, EXPERTS), jnp.float32)
    spread = spread * D ** (-0.5)
    return jnp.clip(spread, -4.0, 4.0).astype(jnp.bfloat16)


def block_scale(stream_key, extent, split, least, top_value):
    def one(dim, shards_of):
        steps = jax.random.uniform(jax.random.fold_in(jax.random.fold_in(stream_key, 6), dim), (shards_of,), jnp.float32, least / len(split), top_value / len(split))
        return jnp.repeat(jnp.exp(steps), extent[dim] // shards_of).reshape((-1,) + (1,) * (len(extent) - dim - 1))

    factor_of = one(*split[0])
    for cut in split[1:]:
        factor_of = factor_of * one(*cut)
    return factor_of


def assign_block(own_key, own, number, rows, amount, top, limit, lean):
    order = jax.random.permutation(own_key, amount)
    packed, common = portions_of(amount, rows * top, limit, lean, True), portions_of(amount, rows * top, limit, lean, False)
    places = jnp.arange(amount)

    def named(sizes, turn):
        used = int((sizes > 0).sum())
        fixed = max(1, used // 4)
        moved = fixed + (places - fixed + turn * (used - fixed)) % max(1, amount - fixed)
        return jnp.zeros((amount,), jnp.int32).at[order[jnp.where(places < fixed, places, moved)]].set(jnp.asarray(sizes, jnp.int32))

    sizes = jnp.where(number % 4 == 0, named(packed, number // 4), named(common, number - number // 4 - 1))
    mixed = jax.random.permutation(jax.random.fold_in(own, 3), amount)
    source_of, sink = mixed[0:amount // 2 * 2:2], mixed[1:amount // 2 * 2:2]
    room = jnp.minimum(sizes[source_of] - 1, limit - sizes[sink]) // 2
    room = jnp.where((source_of == order[0]) | (sink == order[0]) | (sizes[sink] == 0), 0, jnp.maximum(room, 0))
    moved = jax.random.randint(jax.random.fold_in(own, 4), (amount // 2,), 0, 1 << 20) % (room + 1)
    sizes = sizes.at[source_of].add(-moved).at[sink].add(moved)
    items = jnp.searchsorted(jnp.cumsum(sizes), jnp.arange(rows * top), side="right").astype(jnp.int32)
    listing = items.reshape(top, rows).T
    listing = listing[jax.random.permutation(jax.random.fold_in(own, 1), rows)]
    turn = jax.random.randint(jax.random.fold_in(own, 2), (rows, 1), 0, top)
    return jnp.take_along_axis(listing, (jnp.arange(top)[None, :] + turn) % top, axis=1)


def portions_of(amount, total, limit, slope, full):
    weights = [(1 << 20) // math.isqrt(rank ** slope) + 1 for rank in range(1, amount + 1)]
    largest = limit if full else min(limit, max(-(-total // amount), total * weights[0] // sum(weights)))
    least = 1 if total - largest >= amount - 1 else 0
    counts, spare = [largest] + [least] * (amount - 1), total - largest - least * (amount - 1)
    while spare > 0:
        free = [i for i in range(1, amount) if counts[i] < largest] or [i for i in range(1, amount) if counts[i] < limit]
        whole, left = sum([weights[i] for i in free]), spare
        for i in free:
            addition = min(limit - counts[i], max(1, left * weights[i] // whole), spare)
            counts[i] = counts[i] + addition
            spare = spare - addition
    return np.array(counts)


def scatter_about(stream_key, extent, deviation, most, cuts=(), held_as=jnp.bfloat16):
    entries = deviation * jax.random.normal(stream_key, extent, jnp.float32)
    if cuts:
        entries = entries * block_scale(stream_key, extent, cuts, -0.22, 0.18)
    return jnp.clip(entries, -most, most).astype(held_as)


def setup_inputs(seed: int = 0, part: int = 0) -> dict:
    seeds = jax.random.split(jax.random.key(seed), 14)
    own_keys = jax.random.split(jax.random.fold_in(seeds[13], part), 14)
    queries = scatter_about(own_keys[0], (BLOCKS, BLOCK, SEQS, HEADS * HD), 1.0, 6.0, ((0, 4), (3, 4)))
    keys = scatter_about(own_keys[1], (BLOCKS, BLOCK, SEQS, KV_HEADS * HD), 1.0, 6.0, ((0, 4), (3, 4)))
    values = scatter_about(own_keys[2], (BLOCKS, BLOCK, SEQS, KV_HEADS * HD), 2.0, 12.0, ((0, 4), (3, 4)))
    q_gain = draw_q_gain(jax.random.fold_in(seeds[13], 71), part)
    k_gain = draw_k_gain(jax.random.fold_in(seeds[13], 71), part)
    out_weight = scatter_about(seeds[5], (HEADS * HD, D), (HEADS * HD) ** -0.5, 0.09375, ((0, 4), (1, 4)))
    hidden_in = scatter_about(own_keys[6], (BLOCKS, BLOCK, SEQS, D), 0.5, 3.0, ((0, 4), (1, 4)))
    norm_gain = jnp.clip(1.0 + 0.18 * jax.random.normal(seeds[7], (D,), jnp.float32), 0.1, 1.9)
    router = draw_router(jax.random.fold_in(seeds[13], 71), part)
    expert_ids_keys = jax.random.split(jax.random.fold_in(own_keys[9], 1), BLOCKS * BLOCK * SEQS // ROWS_DEV)
    expert_ids_turns = jax.random.permutation(jax.random.fold_in(own_keys[9], 3), BLOCKS * BLOCK * SEQS // ROWS_DEV)
    expert_ids = jax.vmap(lambda own, number: assign_block(jax.random.fold_in(own_keys[9], 2), own, number, ROWS_DEV, EXPERTS, TOPK, CAP, 2))(expert_ids_keys, expert_ids_turns).reshape((BLOCKS, BLOCK, SEQS, TOPK))
    w_gate = scatter_about(seeds[10], (EXPERTS, D, FF), D ** -0.5, 0.09375, ((0, 16),))
    w_up = scatter_about(seeds[11], (EXPERTS, D, FF), D ** -0.5, 0.09375, ((0, 16),))
    w_down = scatter_about(seeds[12], (EXPERTS, FF, D), FF ** -0.5, 0.21875, ((0, 16),))
    return {"queries": queries, "keys": keys, "values": values, "q_gain": q_gain, "k_gain": k_gain, "out_weight": out_weight, "hidden_in": hidden_in, "norm_gain": norm_gain, "router": router, "expert_ids": expert_ids, "w_gate": w_gate, "w_up": w_up, "w_down": w_down}


theta_base = 1000000.0
eps_norm = 1e-06
neg_fill = -1e+30

def head_norm(values_in, gain_vec):
    scale_row = lax.rsqrt(lax.optimization_barrier(jnp.mean(values_in * values_in, axis=-1, keepdims=True)) + eps_norm)
    return values_in * scale_row * gain_vec

def rotary(values_in, places):
    width_all = values_in.shape[-1]
    half_width = width_all // 2
    frequency = theta_base ** (-2.0 * jnp.arange(half_width, dtype=jnp.float32) / width_all)
    angles = places.astype(jnp.float32)[:, None] * frequency[None, :]
    tile_shape = (places.shape[0],) + (1,) * (values_in.ndim - 2) + (half_width,)
    cosine = jnp.cos(angles).reshape(tile_shape)
    sine_part = jnp.sin(angles).reshape(tile_shape)
    first_half = values_in[..., :half_width]
    second = values_in[..., half_width:]
    return jnp.concatenate([first_half * cosine - second * sine_part, second * cosine + first_half * sine_part], axis=-1)

def reference(queries, keys, values, q_gain, k_gain, out_weight, hidden_in, norm_gain, router, expert_ids, w_gate, w_up, w_down):
    length_all = BLOCKS * BLOCK
    group_size = HEADS // KV_HEADS
    score_scale = HD ** (-0.5)
    places = jnp.arange(length_all, dtype=jnp.int32)
    q_field = queries.reshape(length_all, SEQS, HEADS, HD).astype(jnp.float32)
    k_field = keys.reshape(length_all, SEQS, KV_HEADS, HD).astype(jnp.float32)
    q_ready = rotary(head_norm(q_field, q_gain), places).astype(jnp.bfloat16).reshape(length_all, SEQS, KV_HEADS, group_size, HD)
    k_ready = lax.optimization_barrier(rotary(head_norm(k_field, k_gain), places).astype(jnp.bfloat16)).astype(jnp.float32)
    v_all = values.reshape(length_all, SEQS, KV_HEADS, HD).astype(jnp.float32)
    step_len = math.gcd(length_all, 128)
    block_count = length_all // step_len

    def one_block(block_index):
        q_block = lax.optimization_barrier(lax.dynamic_slice_in_dim(q_ready, block_index * step_len, step_len, 0)).astype(jnp.float32)
        scores = jnp.einsum('pskgd,nskd->skgpn', q_block, k_ready) * score_scale
        q_places = block_index * step_len + jnp.arange(step_len, dtype=jnp.int32)
        allowed = places[None, :] <= q_places[:, None]
        scores = jnp.where(allowed, scores, neg_fill)
        row_top = lax.optimization_barrier(jnp.max(scores, axis=-1, keepdims=True))
        weights = jnp.where(allowed, jnp.exp(scores - row_top), 0.0)
        total_sum = lax.optimization_barrier(jnp.sum(weights, axis=-1))
        rounded = lax.optimization_barrier(weights.astype(jnp.bfloat16)).astype(jnp.float32)
        mixed_rows = jnp.einsum('skgpn,nskd->pskgd', rounded, v_all) / jnp.transpose(total_sum, (3, 0, 1, 2))[..., None]
        return mixed_rows.astype(jnp.bfloat16)
    attended = lax.map(one_block, jnp.arange(block_count, dtype=jnp.int32))
    row_count = length_all * SEQS
    attended = attended.reshape(row_count, HEADS * HD)
    projected = jnp.dot(attended, out_weight, preferred_element_type=jnp.float32)
    stream = (hidden_in.reshape(row_count, D).astype(jnp.float32) + projected).astype(jnp.bfloat16)
    stream_f = stream.astype(jnp.float32)
    normed = (stream_f * lax.rsqrt(lax.optimization_barrier(jnp.mean(stream_f * stream_f, axis=-1, keepdims=True)) + eps_norm) * norm_gain).astype(jnp.bfloat16)
    logits = jnp.dot(normed, router, preferred_element_type=jnp.float32)
    chosen = expert_ids.reshape(row_count, TOPK)
    catalog = jnp.arange(EXPERTS, dtype=jnp.int32)
    chosen_mask = chosen[:, :, None] == catalog[None, None, :]
    picked = lax.optimization_barrier(jnp.sum(jnp.where(chosen_mask, logits[:, None, :], 0.0), axis=-1))
    gate_weights = jax.nn.softmax(picked, axis=-1)
    pair_count = ROWS_DEV * TOPK
    device_blocks = row_count // ROWS_DEV
    grouped = chosen.reshape(device_blocks, pair_count)

    def slot_block(ids_row):
        hit_table = (ids_row[:, None] == catalog[None, :]).astype(jnp.int32)
        return lax.optimization_barrier(jnp.sum((jnp.cumsum(hit_table, axis=0) - hit_table) * hit_table, axis=1))
    slot_index = lax.map(slot_block, grouped)
    owners = jnp.arange(device_blocks, dtype=jnp.int32)[:, None] * CAP + slot_index
    total_pairs = row_count * TOPK
    pair_ids = jnp.arange(total_pairs, dtype=jnp.int32).reshape(device_blocks, pair_count)
    table = jnp.full((EXPERTS, device_blocks * CAP), total_pairs, jnp.int32).at[grouped, owners].set(pair_ids)
    normed_pad = jnp.concatenate([normed, jnp.zeros((1, D), jnp.bfloat16)], axis=0)
    gates_pad = jnp.concatenate([gate_weights.reshape(total_pairs), jnp.zeros((1,), jnp.float32)], axis=0)

    def per_expert(accum_state, expert):
        pair_pick = table[expert]
        row_index = (pair_pick // TOPK).astype(jnp.int32)
        inputs = normed_pad[row_index]
        gate_part = jnp.dot(inputs, w_gate[expert], preferred_element_type=jnp.float32)
        up_part = jnp.dot(inputs, w_up[expert], preferred_element_type=jnp.float32)
        inner_act = (jax.nn.silu(gate_part) * up_part).astype(jnp.bfloat16)
        expert_out = lax.optimization_barrier(jnp.dot(inner_act, w_down[expert], preferred_element_type=jnp.float32).astype(jnp.bfloat16)).astype(jnp.float32)
        accum_state = accum_state.at[row_index].add(gates_pad[pair_pick][:, None] * expert_out)
        return (accum_state, None)
    blended, _ = lax.scan(per_expert, jnp.zeros((row_count + 1, D), jnp.float32), jnp.arange(EXPERTS, dtype=jnp.int32))
    final_rows = (stream_f + blended[:row_count]).astype(jnp.bfloat16)
    return final_rows.reshape(BLOCKS, BLOCK, SEQS, D)
```

```python
import jax
import jax.numpy as jnp
from jax import lax
from jax.sharding import PartitionSpec as P

theta_base = 1000000.0
eps_norm = 1e-06
neg_fill = -1e30
chunk_count = 2


def head_norm(values_in, gain_vec):
    scale_row = lax.rsqrt(jnp.mean(values_in * values_in, axis=-1, keepdims=True) + eps_norm)
    return values_in * scale_row * gain_vec


def rotary(values_in, places):
    width_all = values_in.shape[-1]
    half_width = width_all // 2
    frequency = theta_base ** (-2.0 * jnp.arange(half_width, dtype=jnp.float32) / width_all)
    angles = places.astype(jnp.float32)[:, None] * frequency[None, :]
    tile_shape = (places.shape[0],) + (1,) * (values_in.ndim - 2) + (half_width,)
    cosine = jnp.cos(angles).reshape(tile_shape)
    sine_part = jnp.sin(angles).reshape(tile_shape)
    first_half = values_in[..., :half_width]
    second = values_in[..., half_width:]
    return jnp.concatenate(
        [first_half * cosine - second * sine_part, second * cosine + first_half * sine_part],
        axis=-1,
    )


def attend(
    carry_state,
    query_set,
    query_places,
    low_bound,
    high_bound,
    key_piece,
    value_piece,
    start_row,
    score_scale,
):
    piece_len = key_piece.shape[0]
    key_places = jnp.arange(piece_len, dtype=jnp.int32)

    def compute(carry_inner):
        max_old, total_old, accum_old = carry_inner
        scores = (
            jnp.einsum(
                "pskgd,nskd->skgpn", query_set, key_piece, preferred_element_type=jnp.float32
            )
            * score_scale
        )
        allowed = (
            (key_places[None, :] <= query_places[:, None])
            & (key_places[None, :] >= low_bound)
            & (key_places[None, :] < high_bound)
        )
        scores = jnp.where(allowed, scores, neg_fill)
        max_new = jnp.maximum(max_old, jnp.max(scores, axis=-1))
        weights = jnp.where(allowed, jnp.exp(scores - max_new[..., None]), 0.0)
        total_new = jnp.sum(weights, axis=-1)
        accum_new = jnp.einsum(
            "skgpn,nskd->skgpd",
            weights.astype(jnp.bfloat16),
            value_piece,
            preferred_element_type=jnp.float32,
        )
        return (max_new, total_new, accum_new)

    live_piece = (
        (start_row <= jnp.max(query_places))
        & (start_row < high_bound)
        & (start_row + piece_len > low_bound)
    )
    return lax.cond(live_piece, compute, lambda carry_inner: carry_inner, carry_state)


def on_device(
    queries,
    keys,
    values,
    q_gain,
    k_gain,
    out_weight,
    hidden_in,
    norm_gain,
    router,
    expert_ids,
    w_gate,
    w_up,
    w_down,
):
    split_count = lax.axis_size("expert")
    tensor_count = lax.axis_size("tensor")
    place_index = lax.axis_index("expert")
    block_len = queries.shape[1]
    seq_count = queries.shape[2]
    head_dim = q_gain.shape[0]
    head_count = queries.shape[3] // head_dim
    kv_count = keys.shape[3] // head_dim
    group_size = head_count // kv_count
    score_scale = head_dim ** (-0.5)
    offsets = jnp.arange(block_len, dtype=jnp.int32)
    q_places = place_index * block_len + offsets
    q_field = queries[0].astype(jnp.float32).reshape(block_len, seq_count, head_count, head_dim)
    q_ready = (
        rotary(head_norm(q_field, q_gain), q_places)
        .astype(jnp.bfloat16)
        .reshape(block_len, seq_count, kv_count, group_size, head_dim)
    )
    k_field = keys[0].astype(jnp.float32).reshape(block_len, seq_count, kv_count, head_dim)
    k_ready = rotary(head_norm(k_field, k_gain), q_places).astype(jnp.bfloat16)
    v_ready = values[0].reshape(block_len, seq_count, kv_count, head_dim)
    stat_shape = (seq_count, kv_count, group_size, block_len)
    fresh_state = (
        jnp.full(stat_shape, neg_fill, jnp.float32),
        jnp.zeros(stat_shape, jnp.float32),
        jnp.zeros(stat_shape + (head_dim,), jnp.float32),
    )
    own_high = place_index * block_len + block_len
    kv_pack = lax.all_gather(
        jnp.concatenate([k_ready, v_ready], axis=-1), "expert", axis=0, tiled=True
    )
    folded = attend(
        fresh_state,
        q_ready,
        q_places,
        0,
        own_high,
        kv_pack[..., :head_dim],
        kv_pack[..., head_dim:],
        jnp.int32(0),
        score_scale,
    )
    max_all, total_all, accum_all = folded
    attended = (accum_all / total_all[..., None]).astype(jnp.bfloat16)
    attn_rows = jnp.transpose(attended, (3, 0, 1, 2, 4)).reshape(
        block_len * seq_count, head_count * head_dim
    )
    share = out_weight.shape[1] // lax.axis_size("dp")
    own_share = lax.dynamic_slice_in_dim(out_weight, lax.axis_index("dp") * share, share, 1)
    weight_parts = lax.all_gather(own_share, ("expert", "dp"), axis=0, tiled=False)
    partial_value = jnp.einsum(
        "rc,gcn->rgn", attn_rows, weight_parts, preferred_element_type=jnp.float32
    ).reshape(attn_rows.shape[0], -1)
    mixed_rows = lax.psum_scatter(
        partial_value.astype(jnp.bfloat16), "tensor", scatter_dimension=0, tiled=True
    ).astype(jnp.float32)
    d_model = hidden_in.shape[3]
    row_count = hidden_in.shape[1] * seq_count
    stream = (hidden_in.reshape(row_count, d_model).astype(jnp.float32) + mixed_rows).astype(
        jnp.bfloat16
    )
    stream_f = stream.astype(jnp.float32)
    normed = (
        stream_f
        * lax.rsqrt(jnp.mean(stream_f * stream_f, axis=-1, keepdims=True) + eps_norm)
        * norm_gain
    ).astype(jnp.bfloat16)
    local_experts = w_gate.shape[0]
    device_count = tensor_count * split_count
    experts = local_experts * device_count
    top_count = expert_ids.shape[3]
    spread = ("tensor", "expert")
    chosen = lax.all_gather(expert_ids.reshape(row_count, top_count), spread, axis=0)
    catalog = jnp.arange(experts, dtype=jnp.int32)
    first_expert = (lax.axis_index("tensor") * split_count + place_index) * local_experts
    piece_rows = row_count // chunk_count
    blended = []
    for chunk in range(chunk_count):
        span = slice(chunk * piece_rows, (chunk + 1) * piece_rows)
        rows = lax.all_gather(normed[span], spread, axis=0, tiled=True)
        ids = chosen[:, span].reshape(-1, top_count)
        named = jnp.any(ids[:, :, None] == catalog[None, None, :], axis=1)
        logits = jnp.dot(rows, router, preferred_element_type=jnp.float32)
        top_logit = jnp.max(jnp.where(named, logits, -jnp.inf), axis=-1, keepdims=True)
        odds = jnp.where(named, jnp.exp(jnp.where(named, logits - top_logit, 0.0)), 0.0)
        gates = odds / jnp.sum(odds, axis=-1, keepdims=True)
        share_sum = 0.0
        for local in range(local_experts):
            gate_part = jnp.dot(rows, w_gate[local], preferred_element_type=jnp.float32)
            up_part = jnp.dot(rows, w_up[local], preferred_element_type=jnp.float32)
            inner_act = (jax.nn.silu(gate_part) * up_part).astype(jnp.bfloat16)
            expert_rows = jnp.dot(
                inner_act, w_down[local], preferred_element_type=jnp.float32
            ).astype(jnp.bfloat16)
            own_gate = jnp.sum(
                jnp.where(catalog == first_expert + local, gates, 0.0), axis=-1, keepdims=True
            )
            share_sum = share_sum + own_gate * expert_rows.astype(jnp.float32)
        blended.append(
            lax.psum_scatter(
                share_sum.astype(jnp.bfloat16), spread, scatter_dimension=0, tiled=True
            )
        )
    blended = jnp.concatenate(blended, axis=0).astype(jnp.float32)
    final_rows = (stream_f + blended).astype(jnp.bfloat16)
    return final_rows.reshape(hidden_in.shape)


def solution(mesh):
    return jax.shard_map(
        on_device,
        mesh=mesh,
        in_specs=(
            P(("dp", "expert"), None, None, "tensor"),
            P(("dp", "expert"), None, None, "tensor"),
            P(("dp", "expert"), None, None, "tensor"),
            P(),
            P(),
            P("tensor", "expert"),
            P(("dp", "expert"), "tensor", None, None),
            P(),
            P(),
            P(("dp", "expert"), "tensor", None, None),
            P(("tensor", "expert"), None, None),
            P(("tensor", "expert"), None, None),
            P(("tensor", "expert"), None, None),
        ),
        out_specs=P(("dp", "expert"), "tensor", None, None),
        check_vma=False,
    )
```

```python
import jax
import jax.numpy as jnp
from jax import lax
from jax.sharding import PartitionSpec as P

theta_base = 1000000.0
eps_norm = 1e-06
neg_fill = -1e30
chunk_count = 2


def head_norm(values_in, gain_vec):
    scale_row = lax.rsqrt(jnp.mean(values_in * values_in, axis=-1, keepdims=True) + eps_norm)
    return values_in * scale_row * gain_vec


def rotary(values_in, places):
    width_all = values_in.shape[-1]
    half_width = width_all // 2
    frequency = theta_base ** (-2.0 * jnp.arange(half_width, dtype=jnp.float32) / width_all)
    angles = places.astype(jnp.float32)[:, None] * frequency[None, :]
    tile_shape = (places.shape[0],) + (1,) * (values_in.ndim - 2) + (half_width,)
    cosine = jnp.cos(angles).reshape(tile_shape)
    sine_part = jnp.sin(angles).reshape(tile_shape)
    first_half = values_in[..., :half_width]
    second = values_in[..., half_width:]
    return jnp.concatenate(
        [first_half * cosine - second * sine_part, second * cosine + first_half * sine_part],
        axis=-1,
    )


def attend(
    carry_state,
    query_set,
    query_places,
    low_bound,
    high_bound,
    key_piece,
    value_piece,
    start_row,
    score_scale,
):
    piece_len = key_piece.shape[0]
    key_places = jnp.arange(piece_len, dtype=jnp.int32)

    def compute(carry_inner):
        max_old, total_old, accum_old = carry_inner
        scores = (
            jnp.einsum(
                "pskgd,nskd->skgpn", query_set, key_piece, preferred_element_type=jnp.float32
            )
            * score_scale
        )
        allowed = (
            (key_places[None, :] <= query_places[:, None])
            & (key_places[None, :] >= low_bound)
            & (key_places[None, :] < high_bound)
        )
        scores = jnp.where(allowed, scores, neg_fill)
        max_new = jnp.maximum(max_old, jnp.max(scores, axis=-1))
        weights = jnp.where(allowed, jnp.exp(scores - max_new[..., None]), 0.0)
        total_new = jnp.sum(weights, axis=-1)
        accum_new = jnp.einsum(
            "skgpn,nskd->skgpd",
            weights.astype(jnp.bfloat16),
            value_piece,
            preferred_element_type=jnp.float32,
        )
        return (max_new, total_new, accum_new)

    live_piece = (
        (start_row <= jnp.max(query_places))
        & (start_row < high_bound)
        & (start_row + piece_len > low_bound)
    )
    return lax.cond(live_piece, compute, lambda carry_inner: carry_inner, carry_state)


def fold_halves(total, name, dim):
    members = total.shape[dim]
    place = lax.axis_index(name)
    step = 1
    while step < members:
        shape = total.shape
        total = total.reshape(shape[:dim] + (shape[dim] // 2, 2) + shape[dim + 1 :])
        bit = (place // step) % 2
        keep = lax.dynamic_index_in_dim(total, bit, dim + 1, keepdims=False)
        send = lax.dynamic_index_in_dim(total, 1 - bit, dim + 1, keepdims=False)
        got = lax.ppermute(send, name, [(i, i ^ step) for i in range(members)])
        total = (keep.astype(jnp.float32) + got.astype(jnp.float32)).astype(total.dtype)
        step *= 2
    return total


def sum_to_owner(rows, tensor_count, split_count):
    if tensor_count & (tensor_count - 1) or split_count & (split_count - 1):
        return lax.psum_scatter(rows, ("tensor", "expert"), scatter_dimension=0, tiled=True)
    total = rows.reshape(tensor_count, split_count, -1, rows.shape[1])
    total = fold_halves(total, "tensor", 0)
    total = fold_halves(total, "expert", 1)
    return total.reshape(-1, rows.shape[1])


def on_device(
    queries,
    keys,
    values,
    q_gain,
    k_gain,
    out_weight,
    hidden_in,
    norm_gain,
    router,
    expert_ids,
    w_gate,
    w_up,
    w_down,
):
    split_count = lax.axis_size("expert")
    tensor_count = lax.axis_size("tensor")
    place_index = lax.axis_index("expert")
    block_len = queries.shape[1]
    seq_count = queries.shape[2]
    head_dim = q_gain.shape[0]
    head_count = queries.shape[3] // head_dim
    kv_count = keys.shape[3] // head_dim
    group_size = head_count // kv_count
    score_scale = head_dim ** (-0.5)
    offsets = jnp.arange(block_len, dtype=jnp.int32)
    q_places = place_index * block_len + offsets
    q_field = queries[0].astype(jnp.float32).reshape(block_len, seq_count, head_count, head_dim)
    q_ready = (
        rotary(head_norm(q_field, q_gain), q_places)
        .astype(jnp.bfloat16)
        .reshape(block_len, seq_count, kv_count, group_size, head_dim)
    )
    k_field = keys[0].astype(jnp.float32).reshape(block_len, seq_count, kv_count, head_dim)
    k_ready = rotary(head_norm(k_field, k_gain), q_places).astype(jnp.bfloat16)
    v_ready = values[0].reshape(block_len, seq_count, kv_count, head_dim)
    stat_shape = (seq_count, kv_count, group_size, block_len)
    fresh_state = (
        jnp.full(stat_shape, neg_fill, jnp.float32),
        jnp.zeros(stat_shape, jnp.float32),
        jnp.zeros(stat_shape + (head_dim,), jnp.float32),
    )
    own_high = place_index * block_len + block_len
    folded = attend(
        fresh_state,
        q_ready,
        q_places,
        0,
        own_high,
        lax.all_gather(k_ready, "expert", axis=0, tiled=True),
        lax.all_gather(v_ready, "expert", axis=0, tiled=True),
        jnp.int32(0),
        score_scale,
    )
    max_all, total_all, accum_all = folded
    attended = (accum_all / total_all[..., None]).astype(jnp.bfloat16)
    attn_rows = jnp.transpose(attended, (3, 0, 1, 2, 4)).reshape(
        block_len * seq_count, head_count * head_dim
    )
    share = out_weight.shape[1] // lax.axis_size("dp")
    own_share = lax.dynamic_slice_in_dim(out_weight, lax.axis_index("dp") * share, share, 1)
    weight_parts = lax.all_gather(own_share, ("expert", "dp"), axis=0, tiled=False)
    row_count = hidden_in.shape[1] * seq_count
    top_count = expert_ids.shape[3]
    spread = ("tensor", "expert")
    chosen = lax.all_gather(expert_ids.reshape(row_count, top_count), spread, axis=0)
    attn_rows, chosen = lax.optimization_barrier((attn_rows, chosen))
    partial_value = jnp.concatenate(
        [
            jnp.dot(attn_rows, weight_parts[part], preferred_element_type=jnp.float32).astype(
                jnp.bfloat16
            )
            for part in range(weight_parts.shape[0])
        ],
        axis=1,
    )
    mixed_rows = lax.psum_scatter(
        partial_value, "tensor", scatter_dimension=0, tiled=True
    ).astype(jnp.float32)
    d_model = hidden_in.shape[3]
    stream = (hidden_in.reshape(row_count, d_model).astype(jnp.float32) + mixed_rows).astype(
        jnp.bfloat16
    )
    stream_f = stream.astype(jnp.float32)
    normed = (
        stream_f
        * lax.rsqrt(jnp.mean(stream_f * stream_f, axis=-1, keepdims=True) + eps_norm)
        * norm_gain
    ).astype(jnp.bfloat16)
    local_experts = w_gate.shape[0]
    device_count = tensor_count * split_count
    experts = local_experts * device_count
    catalog = jnp.arange(experts, dtype=jnp.int32)
    first_expert = (lax.axis_index("tensor") * split_count + place_index) * local_experts
    piece_rows = row_count // chunk_count
    blended = []
    for chunk in range(chunk_count):
        span = slice(chunk * piece_rows, (chunk + 1) * piece_rows)
        rows = lax.all_gather(normed[span], spread, axis=0, tiled=True)
        if chunk > 0:
            rows, _ = lax.optimization_barrier((rows, share_sum))
        ids = chosen[:, span].reshape(-1, top_count)
        named = jnp.any(ids[:, :, None] == catalog[None, None, :], axis=1)
        logits = jnp.dot(rows, router, preferred_element_type=jnp.float32)
        top_logit = jnp.max(jnp.where(named, logits, -jnp.inf), axis=-1, keepdims=True)
        odds = jnp.where(named, jnp.exp(jnp.where(named, logits - top_logit, 0.0)), 0.0)
        gates = odds / jnp.sum(odds, axis=-1, keepdims=True)
        share_sum = 0.0
        for local in range(local_experts):
            gate_part = jnp.dot(rows, w_gate[local], preferred_element_type=jnp.float32)
            up_part = jnp.dot(rows, w_up[local], preferred_element_type=jnp.float32)
            inner_act = (jax.nn.silu(gate_part) * up_part).astype(jnp.bfloat16)
            expert_rows = jnp.dot(
                inner_act, w_down[local], preferred_element_type=jnp.float32
            ).astype(jnp.bfloat16)
            own_gate = jnp.sum(
                jnp.where(catalog == first_expert + local, gates, 0.0), axis=-1, keepdims=True
            )
            share_sum = share_sum + own_gate * expert_rows.astype(jnp.float32)
        share_sum = share_sum.astype(jnp.bfloat16)
        blended.append(sum_to_owner(share_sum, tensor_count, split_count))
    blended = jnp.concatenate(blended, axis=0).astype(jnp.float32)
    final_rows = (stream_f + blended).astype(jnp.bfloat16)
    return final_rows.reshape(hidden_in.shape)


def solution(mesh):
    return jax.shard_map(
        on_device,
        mesh=mesh,
        in_specs=(
            P(("dp", "expert"), None, None, "tensor"),
            P(("dp", "expert"), None, None, "tensor"),
            P(("dp", "expert"), None, None, "tensor"),
            P(),
            P(),
            P("tensor", "expert"),
            P(("dp", "expert"), "tensor", None, None),
            P(),
            P(),
            P(("dp", "expert"), "tensor", None, None),
            P(("tensor", "expert"), None, None),
            P(("tensor", "expert"), None, None),
            P(("tensor", "expert"), None, None),
        ),
        out_specs=P(("dp", "expert"), "tensor", None, None),
        check_vma=False,
    )
```

```python
import jax
import jax.numpy as jnp
from jax import lax
from jax.sharding import PartitionSpec as P

theta_base = 1000000.0
eps_norm = 1e-06
neg_fill = -1e30
chunk_plan = ((0, 2, True), (2, 1, True), (3, 1, False))


def head_norm(values_in, gain_vec):
    scale_row = lax.rsqrt(jnp.mean(values_in * values_in, axis=-1, keepdims=True) + eps_norm)
    return values_in * scale_row * gain_vec


def rotary(values_in, places):
    width_all = values_in.shape[-1]
    half_width = width_all // 2
    frequency = theta_base ** (-2.0 * jnp.arange(half_width, dtype=jnp.float32) / width_all)
    angles = places.astype(jnp.float32)[:, None] * frequency[None, :]
    tile_shape = (places.shape[0],) + (1,) * (values_in.ndim - 2) + (half_width,)
    cosine = jnp.cos(angles).reshape(tile_shape)
    sine_part = jnp.sin(angles).reshape(tile_shape)
    first_half = values_in[..., :half_width]
    second = values_in[..., half_width:]
    return jnp.concatenate(
        [first_half * cosine - second * sine_part, second * cosine + first_half * sine_part],
        axis=-1,
    )


def attend(
    carry_state,
    query_set,
    query_places,
    low_bound,
    high_bound,
    key_piece,
    value_piece,
    start_row,
    score_scale,
):
    piece_len = key_piece.shape[0]
    key_places = jnp.arange(piece_len, dtype=jnp.int32)

    def compute(carry_inner):
        max_old, total_old, accum_old = carry_inner
        scores = (
            jnp.einsum(
                "pskgd,nskd->skgpn", query_set, key_piece, preferred_element_type=jnp.float32
            )
            * score_scale
        )
        allowed = (
            (key_places[None, :] <= query_places[:, None])
            & (key_places[None, :] >= low_bound)
            & (key_places[None, :] < high_bound)
        )
        scores = jnp.where(allowed, scores, neg_fill)
        max_new = jnp.maximum(max_old, jnp.max(scores, axis=-1))
        weights = jnp.where(allowed, jnp.exp(scores - max_new[..., None]), 0.0)
        total_new = jnp.sum(weights, axis=-1)
        accum_new = jnp.einsum(
            "skgpn,nskd->skgpd",
            weights.astype(jnp.bfloat16),
            value_piece,
            preferred_element_type=jnp.float32,
        )
        return (max_new, total_new, accum_new)

    live_piece = (
        (start_row <= jnp.max(query_places))
        & (start_row < high_bound)
        & (start_row + piece_len > low_bound)
    )
    return lax.cond(live_piece, compute, lambda carry_inner: carry_inner, carry_state)


def fold_half(total, name, dim, step):
    place = lax.axis_index(name)
    shape = total.shape
    total = total.reshape(shape[:dim] + (shape[dim] // 2, 2) + shape[dim + 1 :])
    bit = (place // step) % 2
    keep = lax.dynamic_index_in_dim(total, bit, dim + 1, keepdims=False)
    send = lax.dynamic_index_in_dim(total, 1 - bit, dim + 1, keepdims=False)
    pairs = [(i, i ^ step) for i in range(lax.axis_size(name))]
    got = lax.ppermute(send, name, pairs)
    return (keep.astype(jnp.float32) + got.astype(jnp.float32)).astype(total.dtype)


def sum_to_owner(rows, tensor_count, split_count):
    if tensor_count & (tensor_count - 1) or split_count & (split_count - 1):
        done = lax.psum_scatter(rows, ("tensor", "expert"), scatter_dimension=0, tiled=True)
        return rows, rows, done
    total = rows.reshape(tensor_count, split_count, -1, rows.shape[1])
    near = total
    for level in range(tensor_count.bit_length() - 1):
        total = fold_half(total, "tensor", 0, 1 << level)
        near = total if level == 0 else near
    middle = total
    for level in range(split_count.bit_length() - 1):
        total = fold_half(total, "expert", 1, 1 << level)
    return near, middle, total.reshape(-1, rows.shape[1])


def on_device(
    queries,
    keys,
    values,
    q_gain,
    k_gain,
    out_weight,
    hidden_in,
    norm_gain,
    router,
    expert_ids,
    w_gate,
    w_up,
    w_down,
):
    split_count = lax.axis_size("expert")
    tensor_count = lax.axis_size("tensor")
    place_index = lax.axis_index("expert")
    block_len = queries.shape[1]
    seq_count = queries.shape[2]
    head_dim = q_gain.shape[0]
    head_count = queries.shape[3] // head_dim
    kv_count = keys.shape[3] // head_dim
    group_size = head_count // kv_count
    score_scale = head_dim ** (-0.5)
    offsets = jnp.arange(block_len, dtype=jnp.int32)
    q_places = place_index * block_len + offsets
    q_field = queries[0].astype(jnp.float32).reshape(block_len, seq_count, head_count, head_dim)
    q_ready = (
        rotary(head_norm(q_field, q_gain), q_places)
        .astype(jnp.bfloat16)
        .reshape(block_len, seq_count, kv_count, group_size, head_dim)
    )
    k_field = keys[0].astype(jnp.float32).reshape(block_len, seq_count, kv_count, head_dim)
    k_ready = rotary(head_norm(k_field, k_gain), q_places).astype(jnp.bfloat16)
    v_ready = values[0].reshape(block_len, seq_count, kv_count, head_dim)
    stat_shape = (seq_count, kv_count, group_size, block_len)
    fresh_state = (
        jnp.full(stat_shape, neg_fill, jnp.float32),
        jnp.zeros(stat_shape, jnp.float32),
        jnp.zeros(stat_shape + (head_dim,), jnp.float32),
    )
    own_high = place_index * block_len + block_len
    folded = attend(
        fresh_state,
        q_ready,
        q_places,
        0,
        own_high,
        lax.all_gather(k_ready, "expert", axis=0, tiled=True),
        lax.all_gather(v_ready, "expert", axis=0, tiled=True),
        jnp.int32(0),
        score_scale,
    )
    max_all, total_all, accum_all = folded
    attended = (accum_all / total_all[..., None]).astype(jnp.bfloat16)
    attn_rows = jnp.transpose(attended, (3, 0, 1, 2, 4)).reshape(
        block_len * seq_count, head_count * head_dim
    )
    share = out_weight.shape[1] // lax.axis_size("dp")
    own_share = lax.dynamic_slice_in_dim(out_weight, lax.axis_index("dp") * share, share, 1)
    weight_parts = lax.all_gather(own_share, ("expert", "dp"), axis=0, tiled=False)
    row_count = hidden_in.shape[1] * seq_count
    top_count = expert_ids.shape[3]
    spread = ("tensor", "expert")
    chosen = lax.all_gather(expert_ids.reshape(row_count, top_count), spread, axis=0)
    attn_rows, chosen = lax.optimization_barrier((attn_rows, chosen))
    partial_value = jnp.concatenate(
        [
            jnp.dot(attn_rows, weight_parts[part], preferred_element_type=jnp.float32).astype(
                jnp.bfloat16
            )
            for part in range(weight_parts.shape[0])
        ],
        axis=1,
    )
    mixed_rows = lax.psum_scatter(
        partial_value, "tensor", scatter_dimension=0, tiled=True
    ).astype(jnp.float32)
    d_model = hidden_in.shape[3]
    stream = (hidden_in.reshape(row_count, d_model).astype(jnp.float32) + mixed_rows).astype(
        jnp.bfloat16
    )
    stream_f = stream.astype(jnp.float32)
    normed = (
        stream_f
        * lax.rsqrt(jnp.mean(stream_f * stream_f, axis=-1, keepdims=True) + eps_norm)
        * norm_gain
    ).astype(jnp.bfloat16)
    local_experts = w_gate.shape[0]
    device_count = tensor_count * split_count
    experts = local_experts * device_count
    catalog = jnp.arange(experts, dtype=jnp.int32)
    first_expert = (lax.axis_index("tensor") * split_count + place_index) * local_experts
    piece_rows = row_count // 4
    blended = []
    for chunk, (begin, pieces, fetch) in enumerate(chunk_plan):
        span = slice(begin * piece_rows, (begin + pieces) * piece_rows)
        if fetch:
            wide = slice(begin * piece_rows, (begin + 2) * piece_rows)
            gathered = lax.all_gather(normed[wide], spread, axis=0)
        inside = (begin % 2) * piece_rows
        rows = gathered[:, inside : inside + pieces * piece_rows].reshape(-1, d_model)
        if chunk > 0:
            rows, _ = lax.optimization_barrier((rows, middle if fetch else near))
        ids = chosen[:, span].reshape(-1, top_count)
        named = jnp.any(ids[:, :, None] == catalog[None, None, :], axis=1)
        logits = jnp.dot(rows, router, preferred_element_type=jnp.float32)
        top_logit = jnp.max(jnp.where(named, logits, -jnp.inf), axis=-1, keepdims=True)
        odds = jnp.where(named, jnp.exp(jnp.where(named, logits - top_logit, 0.0)), 0.0)
        gates = odds / jnp.sum(odds, axis=-1, keepdims=True)
        share_sum = 0.0
        for local in range(local_experts):
            gate_part = jnp.dot(rows, w_gate[local], preferred_element_type=jnp.float32)
            up_part = jnp.dot(rows, w_up[local], preferred_element_type=jnp.float32)
            inner_act = (jax.nn.silu(gate_part) * up_part).astype(jnp.bfloat16)
            if chunk > 0 and local == 0:
                inner_act, _ = lax.optimization_barrier((inner_act, middle))
            expert_rows = jnp.dot(
                inner_act, w_down[local], preferred_element_type=jnp.float32
            ).astype(jnp.bfloat16)
            own_gate = jnp.sum(
                jnp.where(catalog == first_expert + local, gates, 0.0), axis=-1, keepdims=True
            )
            share_sum = share_sum + own_gate * expert_rows.astype(jnp.float32)
        share_sum = share_sum.astype(jnp.bfloat16)
        near, middle, done = sum_to_owner(share_sum, tensor_count, split_count)
        blended.append(done)
    blended = jnp.concatenate(blended, axis=0).astype(jnp.float32)
    final_rows = (stream_f + blended).astype(jnp.bfloat16)
    return final_rows.reshape(hidden_in.shape)


def solution(mesh):
    return jax.shard_map(
        on_device,
        mesh=mesh,
        in_specs=(
            P(("dp", "expert"), None, None, "tensor"),
            P(("dp", "expert"), None, None, "tensor"),
            P(("dp", "expert"), None, None, "tensor"),
            P(),
            P(),
            P("tensor", "expert"),
            P(("dp", "expert"), "tensor", None, None),
            P(),
            P(),
            P(("dp", "expert"), "tensor", None, None),
            P(("tensor", "expert"), None, None),
            P(("tensor", "expert"), None, None),
            P(("tensor", "expert"), None, None),
        ),
        out_specs=P(("dp", "expert"), "tensor", None, None),
        check_vma=False,
    )
```
